32 devices in a mesh: occ: 4 (over y, core), vir: 8 (over z, x).
Axes of the slice: x: 2, y: 2, z: 4, core: 2. Of those that a mesh axis runs over, the one named last changes fastest.
Arguments:
- amplitudes: bfloat16 [64, 64, 4096], P('occ', 'vir'), may hold values from -6 to 6
- screen: int32 [64, 64], P('occ', 'vir'), may hold values 0 or 1
- integrals: bfloat16 [4096, 16384], P(None, 'vir'), as said below
Outputs:
- ladder_residual: bfloat16 [64, 64, 128, 128], P('occ', None, 'vir')
The draws below stay inside these ranges and needn't reach their ends.
Inputs may be any that keep to these rules, and one draw needn't show every extreme that they name: integrals[(c, d), (a, b)] equals integrals[(d, c), (b, a)] for all a, b, c, d.
All inputs are finite; a program needn't handle non-finite values. No bound on the sum of `screen` on one device may be relied on, other than what follows from the above.
Results may differ from the reference program's by a relative error of at most 0.0075.
Values may be sent and summed in bfloat16 or wider, within the bound.
A program may use at most 256 MiB of HBM per device.

```python
import jax
import jax.numpy as jnp
from jax import lax

TILE = 64
NOCC = 64
SLAB_VIRT = 128
CDIM = 4096


def draw_integrals(key, part):
    key = jax.random.fold_in(key, 7)
    shape = (SLAB_VIRT, SLAB_VIRT, TILE, TILE)
    base = jax.random.normal(key, shape, jnp.float32)
    paired = (base + jnp.transpose(base, (1, 0, 3, 2))) * (0.70710678 / TILE)
    arranged = jnp.transpose(paired, (2, 3, 0, 1)).reshape(TILE * TILE, SLAB_VIRT * SLAB_VIRT)
    return arranged.astype(jnp.bfloat16)


def place_ends(result, own_key, smallest, largest):
    spot = [jax.random.randint(jax.random.fold_in(own_key, axis), (), 0, length) for axis, length in enumerate(result.shape)]
    widest = result.shape.index(max(result.shape))
    neighbour = spot[:widest] + [(spot[widest] + 1) % result.shape[widest]] + spot[widest + 1:]
    return result.at[tuple(spot)].set(smallest).at[tuple(neighbour)].set(largest)


def steps_of(rng, dims, split, low, largest):
    gain, own = 1.0, jax.random.fold_in(rng, 6)
    for axis_at, blocks in split:
        steps = jnp.exp(jax.random.uniform(jax.random.fold_in(own, axis_at), (blocks,), jnp.float32, low / len(split), largest / len(split)))
        gain = gain * jnp.repeat(steps, dims[axis_at] // blocks).reshape([-1 if axis == axis_at else 1 for axis in range(len(dims))])
    return gain


def noise(key, shape, scale, bound, pieces=(), kind=jnp.bfloat16):
    factor_of = steps_of(key, shape, pieces, -0.22, 0.18) if pieces else 1.0
    result = jax.random.normal(key, shape, jnp.float32) * scale * factor_of
    return jnp.minimum(jnp.maximum(result, -bound), bound).astype(kind)


def setup_inputs(seed: int = 0) -> dict:
    key_list = jax.random.split(jax.random.key(seed), 4)
    return {
        "amplitudes": noise(key_list[0], (NOCC, NOCC, CDIM), 1.0, 6.0, ((0, 4), (1, 8))),
        "screen": place_ends((jax.random.randint(key_list[1], (NOCC, NOCC), 0, 4) < 3).astype(jnp.int32), jax.random.fold_in(key_list[1], 1), 0, 1),
        "integrals": draw_integrals(jax.random.fold_in(key_list[3], 71), 0),
    }


def reference(amplitudes, screen, integrals):
    masked = amplitudes * screen[:, :, None].astype(jnp.bfloat16)

    def row_block(block):
        return jnp.dot(block, integrals, preferred_element_type=jnp.float32)

    ladder = lax.map(row_block, masked)
    ladder = ladder.reshape(NOCC, NOCC, SLAB_VIRT, SLAB_VIRT)
    total = ladder + jnp.transpose(ladder, (1, 0, 3, 2))
    return total.astype(jnp.bfloat16)
```

```python
import jax
import jax.numpy as jnp
from jax import lax
from jax.sharding import PartitionSpec as P

TILE = 64
SLAB_VIRT = 128


def per_device(sizes, amplitudes, screen, integrals):
    n_occ, n_vir = sizes
    masked = amplitudes * screen[:, :, None].astype(jnp.bfloat16)
    rows, cols, cdim = masked.shape
    ratio = rows // cols
    r = lax.rem(lax.axis_index("vir"), ratio)
    parts = masked.reshape(ratio, cols, cols, cdim)
    flipped = jnp.transpose(
        parts.reshape(ratio, cols, cols, TILE, TILE), (0, 2, 1, 4, 3)
    ).reshape(ratio, cols, cols, cdim)
    got = []
    for s in range(ratio):
        pairs = []
        for o in range(n_occ):
            for v in range(n_vir):
                q, rr = divmod(v, ratio)
                pairs.append((o * n_vir + v, q * n_vir + o * ratio + (rr + s) % ratio))
        sent = lax.dynamic_index_in_dim(flipped, lax.rem(r + s, ratio), 0, keepdims=False)
        got.append(lax.ppermute(sent, ("occ", "vir"), pairs))
    stacked = jnp.stack(got)
    order = lax.rem(r - jnp.arange(ratio) + ratio, ratio)
    partner = jnp.take(stacked, order, axis=0)
    local = (parts.astype(jnp.float32) + partner.astype(jnp.float32)).astype(jnp.bfloat16)
    local = local.reshape(rows, cols, cdim)
    whole = lax.all_gather(local, "vir", axis=1, tiled=True)
    out = jnp.einsum("ijc,cn->ijn", whole, integrals, preferred_element_type=jnp.float32)
    return out.astype(jnp.bfloat16).reshape(rows, whole.shape[1], -1, SLAB_VIRT)


def solution(mesh):
    sizes = (mesh.shape["occ"], mesh.shape["vir"])
    return jax.shard_map(
        lambda *args: per_device(sizes, *args),
        mesh=mesh,
        in_specs=(P("occ", "vir", None), P("occ", "vir"), P(None, "vir")),
        out_specs=P("occ", None, "vir", None),
        check_vma=False,
    )
```

```python
import functools

import jax
import jax.numpy as jnp
from jax import lax
from jax.experimental import pallas as pl
from jax.experimental.pallas import tpu as pltpu
from jax.sharding import PartitionSpec as P

TILE = 64
SLAB_VIRT = 128
LINE = 4
CHUNKS = 2
MESH = pl.DeviceIdType.MESH


def exchange_kernel(n_occ, n_vir, main, extra, gathered, turned, local_sem, send_sem, recv_sem, turn_send, turn_recv, extra_send):
    ratio = n_vir // n_occ
    line = LINE if n_vir % LINE == 0 else 1
    wide = n_vir // line
    o, v = lax.axis_index("occ"), lax.axis_index("vir")
    z, x = v // wide, lax.rem(v, wide)
    pairs, cdim = main.shape
    piece = pairs // CHUNKS
    strip = cdim // n_vir
    owner = o * ratio + 1

    barrier = pltpu.get_barrier_semaphore()
    for step in range(1, n_vir):
        pl.semaphore_signal(barrier, inc=1, device_id=(o, lax.rem(v + step, n_vir)), device_id_type=MESH)
    for step in range(1, n_occ):
        pl.semaphore_signal(barrier, inc=1, device_id=(lax.rem(o + step, n_occ), v), device_id_type=MESH)
    pl.semaphore_wait(barrier, n_vir + n_occ - 2)

    def place(source, c):
        if c < CHUNKS:
            return gathered.at[source, pl.ds(c * piece, piece)]
        return gathered.at[n_vir, :, pl.ds(pl.multiple_of(source * strip, strip), strip)]

    def held(source, c, own):
        if own and c < CHUNKS:
            return main.at[pl.ds(c * piece, piece)]
        return place(source, c)

    def along(source, c, own, way, target):
        return pltpu.make_async_remote_copy(
            src_ref=held(source, c, own), dst_ref=place(source, c),
            send_sem=send_sem.at[source, c, way], recv_sem=recv_sem.at[source, c],
            device_id=(o, target), device_id_type=MESH,
        )

    def across(source, c, own):
        return pltpu.make_async_remote_copy(
            src_ref=held(source, c, own),
            dst_ref=turned.at[o, lax.rem(source, ratio), pl.ds(c * piece, piece)],
            send_sem=turn_send.at[source, c],
            recv_sem=turn_recv.at[o, lax.rem(source, ratio), c],
            device_id=(source // ratio, v), device_id_type=MESH,
        )

    waits = []

    def start(cond, make):
        def begin():
            make().start()

        def finish():
            make().wait_send()

        pl.when(cond)(begin)
        waits.append((cond, finish))

    def spread(cond, source, c, own, up, down, sides):
        if up:
            start(cond & (z < line - 1), lambda: along(source, c, own, 0, v + wide))
        if down:
            start(cond & (z > 0), lambda: along(source, c, own, 1, v - wide))
        if sides:
            for step in range(1, wide):
                start(cond, lambda step=step: along(source, c, own, 1 + step, z * wide + lax.rem(x + step, wide)))
        if c < CHUNKS:
            start(cond & (source // ratio != o), lambda: across(source, c, own))

    def arrive(cond, source, c, up, down, sides):
        @pl.when(cond)
        def _():
            along(source, c, False, 0, v).wait_recv()

        spread(cond, source, c, False, up, down, sides)

    always = v >= 0
    keep = pltpu.make_async_copy(main, gathered.at[v], local_sem.at[0])

    def strip_of(target):
        return extra.at[:, pl.ds(pl.multiple_of(target * strip, strip), strip)]

    own_strip = pltpu.make_async_copy(strip_of(v), place(v, CHUNKS), local_sem.at[1])

    def far_strip(step):
        target = lax.rem(v + step, n_vir)
        return pltpu.make_async_remote_copy(
            src_ref=strip_of(target), dst_ref=place(target, CHUNKS),
            send_sem=extra_send.at[step], recv_sem=recv_sem.at[target, CHUNKS],
            device_id=(o, target), device_id_type=MESH,
        )

    for c in range(CHUNKS):
        spread(always, v, c, True, True, True, True)

    @pl.when(v == owner)
    def _():
        own_strip.start()
        for step in range(1, n_vir):
            far_strip(step).start()
        own_strip.wait()

    keep.start()

    @pl.when(v != owner)
    def _():
        along(v, CHUNKS, False, 0, v).wait_recv()

    spread(always, v, CHUNKS, True, True, True, True)

    for d in range(1, line + 1):
        for c in range(CHUNKS + 1):
            if d < line:
                arrive(z >= d, (z - d) * wide + x, c, True, False, True)
                arrive(z < line - d, (z + d) * wide + x, c, False, True, True)
            for step in range(1, wide):
                side = lax.rem(x + step, wide)
                e = d - 1
                arrive(z >= e, (z - e) * wide + side, c, False, False, False)
                if e:
                    arrive(z < line - e, (z + e) * wide + side, c, False, False, False)

    again = pltpu.make_async_copy(gathered.at[n_vir], turned.at[o, 0], local_sem.at[2])
    again.start()
    for step in range(1, n_occ):
        other = lax.rem(o + step, n_occ)
        for k in range(ratio):
            for c in range(CHUNKS):
                pltpu.make_async_remote_copy(
                    src_ref=turned.at[other, k, pl.ds(c * piece, piece)],
                    dst_ref=turned.at[other, k, pl.ds(c * piece, piece)],
                    send_sem=turn_send.at[0, c], recv_sem=turn_recv.at[other, k, c],
                    device_id=(o, v), device_id_type=MESH,
                ).wait_recv()
    for cond, finish in waits:
        pl.when(cond)(finish)

    @pl.when(v == owner)
    def _():
        for step in range(1, n_vir):
            far_strip(step).wait_send()

    keep.wait()
    again.wait()


def exchange(n_occ, n_vir, main, extra):
    pairs, cdim = main.shape
    ratio = n_vir // n_occ
    line = LINE if n_vir % LINE == 0 else 1
    wide = n_vir // line
    return pl.pallas_call(
        functools.partial(exchange_kernel, n_occ, n_vir),
        out_shape=(
            jax.ShapeDtypeStruct((n_vir + 1, pairs, cdim), jnp.bfloat16),
            jax.ShapeDtypeStruct((n_occ, ratio, pairs, cdim), jnp.bfloat16),
        ),
        in_specs=[pl.BlockSpec(memory_space=pl.ANY)] * 2,
        out_specs=(pl.BlockSpec(memory_space=pl.ANY),) * 2,
        scratch_shapes=[
            pltpu.SemaphoreType.DMA((3,)),
            pltpu.SemaphoreType.DMA((n_vir, CHUNKS + 1, wide + 1)),
            pltpu.SemaphoreType.DMA((n_vir, CHUNKS + 1)),
            pltpu.SemaphoreType.DMA((n_vir, CHUNKS)),
            pltpu.SemaphoreType.DMA((n_occ, ratio, CHUNKS)),
            pltpu.SemaphoreType.DMA((n_vir,)),
        ],
        compiler_params=pltpu.CompilerParams(collective_id=0, has_side_effects=True),
    )(main, extra)


def flip(block):
    a, b, cdim = block.shape
    return jnp.transpose(block.reshape(a, b, TILE, TILE), (1, 0, 3, 2)).reshape(b, a, cdim)


def add(a, b):
    return (a.astype(jnp.float32) + b.astype(jnp.float32)).astype(jnp.bfloat16)


def per_device(sizes, amplitudes, screen, integrals):
    n_occ, n_vir = sizes
    rows, cols, cdim = amplitudes.shape
    ratio = rows // cols
    assert ratio == 2 and n_vir == ratio * n_occ
    o, v = lax.axis_index("occ"), lax.axis_index("vir")
    q, r = v // ratio, lax.rem(v, ratio)

    def pick(o, q, r):
        return jnp.where(o < q, r, 1 - r)

    parts = (amplitudes * screen[:, :, None].astype(jnp.bfloat16)).reshape(ratio, cols, cols, cdim)

    def half(k):
        return jnp.where(k == 0, parts[0], parts[1])

    pairs = []
    for a in range(n_occ):
        for b in range(n_vir):
            c, s = divmod(b, ratio)
            t = s if c < a else 1 - s
            pairs.append((a * n_vir + b, c * n_vir + a * ratio + t))
    got = lax.ppermute(half(jnp.where(q < o, r, 1 - r)), ("occ", "vir"), pairs)
    mixed = add(half(pick(o, q, r)), flip(got))
    inner = add(half(r), flip(half(r)))
    main = jnp.where(o == q, inner, mixed)
    gathered, turned = exchange(n_occ, n_vir, main.reshape(cols * cols, cdim), mixed.reshape(cols * cols, cdim))

    width = integrals.shape[1]
    permuted = jnp.transpose(integrals.reshape(TILE, TILE, width), (1, 0, 2)).reshape(cdim, width)
    straight = jnp.dot(gathered.reshape(-1, cdim), integrals, preferred_element_type=jnp.float32)
    crossed = jnp.dot(turned.reshape(-1, cdim), permuted, preferred_element_type=jnp.float32)
    shape = (-1, cols, cols, width // SLAB_VIRT, SLAB_VIRT)
    straight = straight.astype(jnp.bfloat16).reshape(shape)
    crossed = jnp.swapaxes(crossed.astype(jnp.bfloat16).reshape(shape), 1, 2)
    blocks = jnp.concatenate([straight, crossed])
    k = jnp.arange(ratio)[:, None]
    w = jnp.arange(n_vir)[None, :]
    p, s = w // ratio, w % ratio
    first = n_vir + 1
    apart = jnp.where(pick(o, p, s) == k, w, first + p * ratio + k)
    same = jnp.where(k == s, w, jnp.where(k == 0, n_vir, first + o * ratio))
    index = jnp.where(p == o, same, apart)
    out = jnp.take(blocks, index, axis=0, mode="clip")
    return jnp.transpose(out, (0, 2, 1, 3, 4, 5)).reshape(rows, n_vir * cols, -1, SLAB_VIRT)


def solution(mesh):
    sizes = (mesh.shape["occ"], mesh.shape["vir"])
    return jax.shard_map(
        functools.partial(per_device, sizes),
        mesh=mesh,
        in_specs=(P("occ", "vir", None), P("occ", "vir"), P(None, "vir")),
        out_specs=P("occ", None, "vir", None),
        check_vma=False,
    )
```

```python
import functools
import math

import jax
import jax.numpy as jnp
from jax import lax
from jax.experimental import pallas as pl
from jax.experimental.pallas import tpu as pltpu
from jax.sharding import PartitionSpec as P

TILE = 64
SLAB_VIRT = 128
LINE = 4
CHUNKS = 2
STEP = 16
WIDE = 512
NARROW = 256
MESH = pl.DeviceIdType.MESH


def pair_swap(n):
    to = lax.broadcasted_iota(jnp.int32, (n * n, n * n), 0)
    at = lax.broadcasted_iota(jnp.int32, (n * n, n * n), 1)
    hit = (lax.rem(to, n) == at // n) & (to // n == lax.rem(at, n))
    return jnp.where(hit, 1.0, 0.0).astype(jnp.bfloat16)


def exchange_kernel(
    n_occ, n_vir, main, extra, slab, out, gathered, turned, straight, crossed,
    local_sem, send_sem, recv_sem, turn_send, turn_recv, extra_send,
):
    ratio = n_vir // n_occ
    line = LINE if n_vir % LINE == 0 else 1
    wide = n_vir // line
    o, v = lax.axis_index("occ"), lax.axis_index("vir")
    z, x = v // wide, lax.rem(v, wide)
    pairs, cdim = main.shape
    piece = pairs // CHUNKS
    strip = cdim // n_vir
    owner = o * ratio + 1
    cols = out.shape[2]
    width = out.shape[3]
    load = pltpu.make_async_copy(slab, straight, local_sem.at[0])
    load.start()

    barrier = pltpu.get_barrier_semaphore()
    for step in range(1, n_vir):
        pl.semaphore_signal(barrier, inc=1, device_id=(o, lax.rem(v + step, n_vir)), device_id_type=MESH)
    for step in range(1, n_occ):
        pl.semaphore_signal(barrier, inc=1, device_id=(lax.rem(o + step, n_occ), v), device_id_type=MESH)
    pl.semaphore_wait(barrier, n_vir + n_occ - 2)

    def place(source, c):
        if c < CHUNKS:
            return gathered.at[source, pl.ds(c * piece, piece)]
        return gathered.at[n_vir, :, pl.ds(pl.multiple_of(source * strip, strip), strip)]

    def held(source, c, own):
        if own and c < CHUNKS:
            return main.at[pl.ds(c * piece, piece)]
        return place(source, c)

    def along(source, c, own, way, target):
        return pltpu.make_async_remote_copy(
            src_ref=held(source, c, own), dst_ref=place(source, c),
            send_sem=send_sem.at[source, c, way], recv_sem=recv_sem.at[source, c],
            device_id=(o, target), device_id_type=MESH,
        )

    def across(source, c, own):
        return pltpu.make_async_remote_copy(
            src_ref=held(source, c, own),
            dst_ref=turned.at[o, lax.rem(source, ratio), pl.ds(c * piece, piece)],
            send_sem=turn_send.at[source, c],
            recv_sem=turn_recv.at[o, lax.rem(source, ratio), c],
            device_id=(source // ratio, v), device_id_type=MESH,
        )

    waits = []

    def start(cond, make):
        def begin():
            make().start()

        def finish():
            make().wait_send()

        pl.when(cond)(begin)
        waits.append((cond, finish))

    def spread(cond, source, c, own, up, down, sides):
        if up:
            start(cond & (z < line - 1), lambda: along(source, c, own, 0, v + wide))
        if down:
            start(cond & (z > 0), lambda: along(source, c, own, 1, v - wide))
        if sides:
            for step in range(1, wide):
                start(cond, lambda step=step: along(source, c, own, 1 + step, z * wide + lax.rem(x + step, wide)))
        if c < CHUNKS:
            start(cond & (source // ratio != o), lambda: across(source, c, own))

    def arrive(cond, source, c, up, down, sides):
        @pl.when(cond)
        def _():
            along(source, c, False, 0, v).wait_recv()

        spread(cond, source, c, False, up, down, sides)

    always = v >= 0

    def permute(part, count):
        swap = pair_swap(STEP)
        across_c = TILE // STEP

        @pl.loop(part * across_c**2 // count, (part + 1) * across_c**2 // count)
        def _(at):
            c = pl.ds(pl.multiple_of(at // across_c * STEP, STEP), STEP)
            d = pl.ds(pl.multiple_of(lax.rem(at, across_c) * STEP, STEP), STEP)
            for n in range(width // WIDE):
                lanes = pl.ds(n * WIDE, WIDE)
                block = straight[c, d, lanes].reshape(STEP * STEP, WIDE)
                moved = jnp.dot(swap, block, preferred_element_type=jnp.float32)
                crossed[d, c, lanes] = moved.astype(jnp.bfloat16).reshape(STEP, STEP, WIDE)

    def multiply(left, weights, places):
        @pl.loop(0, width // NARROW)
        def _(n):
            lanes = pl.ds(pl.multiple_of(n * NARROW, NARROW), NARROW)
            right = weights[:, :, lanes].reshape(cdim, NARROW)
            got = jnp.dot(left(), right, preferred_element_type=jnp.float32)
            for at, (k, source) in enumerate(places):
                rows = got[at * pairs : (at + 1) * pairs].reshape(cols, cols, NARROW)
                out[pl.ds(k * cols, cols), source, :, lanes] = rows.astype(jnp.bfloat16)

    def row_of(occ, vir):
        q, r = vir // ratio, lax.rem(vir, ratio)
        return jnp.where(occ <= q, r, 1 - r)

    def group(zz):
        sources = [zz * wide + step for step in range(wide)]
        multiply(
            lambda: gathered[pl.ds(zz * wide, wide)].reshape(wide * pairs, cdim),
            straight, [(row_of(o, w), w) for w in sources],
        )

    def strip_of(target):
        return extra.at[:, pl.ds(pl.multiple_of(target * strip, strip), strip)]

    own_strip = pltpu.make_async_copy(strip_of(v), place(v, CHUNKS), local_sem.at[1])

    def far_strip(step):
        target = lax.rem(v + step, n_vir)
        return pltpu.make_async_remote_copy(
            src_ref=strip_of(target), dst_ref=place(target, CHUNKS),
            send_sem=extra_send.at[step], recv_sem=recv_sem.at[target, CHUNKS],
            device_id=(o, target), device_id_type=MESH,
        )

    for c in range(CHUNKS):
        spread(always, v, c, True, True, True, True)

    @pl.when(v == owner)
    def _():
        own_strip.start()
        for step in range(1, n_vir):
            far_strip(step).start()
        own_strip.wait()

    gathered[v] = main[...]

    @pl.when(v != owner)
    def _():
        along(v, CHUNKS, False, 0, v).wait_recv()

    spread(always, v, CHUNKS, True, True, True, True)

    for d in range(1, line + 1):
        for c in range(CHUNKS + 1):
            if d < line:
                arrive(z >= d, (z - d) * wide + x, c, True, False, True)
                arrive(z < line - d, (z + d) * wide + x, c, False, True, True)
            for step in range(1, wide):
                side = lax.rem(x + step, wide)
                e = d - 1
                arrive(z >= e, (z - e) * wide + side, c, False, False, False)
                if e:
                    arrive(z < line - e, (z + e) * wide + side, c, False, False, False)
            if d <= 2 and c < CHUNKS:
                if d == 1 and c == 0:
                    load.wait()
                permute((d - 1) * CHUNKS + c, 2 * CHUNKS)
        if d == 1:
            group(z)
        else:
            pl.when(z >= d - 1)(lambda: group(z - d + 1))
            pl.when(z < line - d + 1)(lambda: group(z + d - 1))

    multiply(lambda: gathered[n_vir], straight, [(0, owner)])
    turned[o, 0] = gathered[n_vir]
    for k in range(1, ratio):
        turned[o, k] = gathered[n_vir]
    for step in range(1, n_occ):
        other = lax.rem(o + step, n_occ)
        for k in range(ratio):
            for c in range(CHUNKS):
                pltpu.make_async_remote_copy(
                    src_ref=turned.at[other, k, pl.ds(c * piece, piece)],
                    dst_ref=turned.at[other, k, pl.ds(c * piece, piece)],
                    send_sem=turn_send.at[0, c], recv_sem=turn_recv.at[other, k, c],
                    device_id=(o, v), device_id_type=MESH,
                ).wait_recv()
    swap = pair_swap(cols)

    @pl.loop(0, n_occ * ratio)
    def _(at):
        p, k = at // ratio, lax.rem(at, ratio)
        moved = jnp.dot(swap, turned[p, k], preferred_element_type=jnp.float32)
        turned[p, k] = moved.astype(jnp.bfloat16)

    places = []
    for p in range(n_occ):
        for k in range(ratio):
            s = jnp.where(p < o, k, 1 - k)
            places.append((jnp.where(p == o, 1, k), p * ratio + jnp.where(p == o, 0, s)))
    multiply(lambda: turned[...].reshape(n_occ * ratio * pairs, cdim), crossed, places)
    for cond, finish in waits:
        pl.when(cond)(finish)

    @pl.when(v == owner)
    def _():
        for step in range(1, n_vir):
            far_strip(step).wait_send()


def ladder(n_occ, n_vir, main, extra, slab):
    pairs, cdim = main.shape
    ratio = n_vir // n_occ
    line = LINE if n_vir % LINE == 0 else 1
    wide = n_vir // line
    cols = math.isqrt(pairs)
    return pl.pallas_call(
        functools.partial(exchange_kernel, n_occ, n_vir),
        out_shape=jax.ShapeDtypeStruct((ratio * cols, n_vir, cols, slab.shape[2]), jnp.bfloat16),
        in_specs=[pl.BlockSpec(memory_space=pltpu.VMEM)] * 2 + [pl.BlockSpec(memory_space=pl.ANY)],
        out_specs=pl.BlockSpec(memory_space=pltpu.VMEM),
        scratch_shapes=[
            pltpu.VMEM((n_vir + 1, pairs, cdim), jnp.bfloat16),
            pltpu.VMEM((n_occ, ratio, pairs, cdim), jnp.bfloat16),
            pltpu.VMEM(slab.shape, jnp.bfloat16),
            pltpu.VMEM(slab.shape, jnp.bfloat16),
            pltpu.SemaphoreType.DMA((2,)),
            pltpu.SemaphoreType.DMA((n_vir, CHUNKS + 1, wide + 1)),
            pltpu.SemaphoreType.DMA((n_vir, CHUNKS + 1)),
            pltpu.SemaphoreType.DMA((n_vir, CHUNKS)),
            pltpu.SemaphoreType.DMA((n_occ, ratio, CHUNKS)),
            pltpu.SemaphoreType.DMA((n_vir,)),
        ],
        compiler_params=pltpu.CompilerParams(
            collective_id=0, has_side_effects=True, vmem_limit_bytes=60 * 2**20
        ),
        cost_estimate=pl.CostEstimate(flops=2**35, bytes_accessed=2**25, transcendentals=0),
    )(main, extra, slab)


def flip(block):
    a, b, cdim = block.shape
    return jnp.transpose(block.reshape(a, b, TILE, TILE), (1, 0, 3, 2)).reshape(b, a, cdim)


def add(a, b):
    return (a.astype(jnp.float32) + b.astype(jnp.float32)).astype(jnp.bfloat16)


def per_device(sizes, amplitudes, screen, integrals):
    n_occ, n_vir = sizes
    rows, cols, cdim = amplitudes.shape
    ratio = rows // cols
    assert ratio == 2 and n_vir == ratio * n_occ
    o, v = lax.axis_index("occ"), lax.axis_index("vir")
    q, r = v // ratio, lax.rem(v, ratio)

    def pick(o, q, r):
        return jnp.where(o < q, r, 1 - r)

    parts = (amplitudes * screen[:, :, None].astype(jnp.bfloat16)).reshape(ratio, cols, cols, cdim)

    def half(k):
        return jnp.where(k == 0, parts[0], parts[1])

    pairs = []
    for a in range(n_occ):
        for b in range(n_vir):
            c, s = divmod(b, ratio)
            t = s if c < a else 1 - s
            pairs.append((a * n_vir + b, c * n_vir + a * ratio + t))
    got = lax.ppermute(half(jnp.where(q < o, r, 1 - r)), ("occ", "vir"), pairs)
    mixed = add(half(pick(o, q, r)), flip(got))
    inner = add(half(r), flip(half(r)))
    main = jnp.where(o == q, inner, mixed)
    width = integrals.shape[1]
    out = ladder(
        n_occ, n_vir, main.reshape(cols * cols, cdim), mixed.reshape(cols * cols, cdim),
        integrals.reshape(TILE, TILE, width),
    )
    return out.reshape(rows, n_vir * cols, -1, SLAB_VIRT)


def solution(mesh):
    sizes = (mesh.shape["occ"], mesh.shape["vir"])
    return jax.shard_map(
        functools.partial(per_device, sizes),
        mesh=mesh,
        in_specs=(P("occ", "vir", None), P("occ", "vir"), P(None, "vir")),
        out_specs=P("occ", None, "vir", None),
        check_vma=False,
    )
```

```python
import functools
import math

import jax
import jax.numpy as jnp
from jax import lax
from jax.experimental import pallas as pl
from jax.experimental.pallas import tpu as pltpu
from jax.sharding import PartitionSpec as P

TILE = 64
SLAB_VIRT = 128
LINE = 4
CHUNKS = 4
PIECES = 2
STEP = 16
WIDE = 512
NARROW = 256
MESH = pl.DeviceIdType.MESH


def pair_swap(n):
    to = lax.broadcasted_iota(jnp.int32, (n * n, n * n), 0)
    at = lax.broadcasted_iota(jnp.int32, (n * n, n * n), 1)
    hit = (lax.rem(to, n) == at // n) & (to // n == lax.rem(at, n))
    return jnp.where(hit, 1.0, 0.0).astype(jnp.bfloat16)


def exchange_kernel(
    n_occ, n_vir, main, extra, slab, out, gathered, turned, straight, crossed,
    local_sem, send_sem, recv_sem, turn_send, turn_recv, extra_send,
):
    ratio = n_vir // n_occ
    line = LINE if n_vir % LINE == 0 else 1
    wide = n_vir // line
    o, v = lax.axis_index("occ"), lax.axis_index("vir")
    z, x = v // wide, lax.rem(v, wide)
    pairs, cdim = main.shape
    piece = pairs // CHUNKS
    strip = cdim // n_vir
    owner = o * ratio + 1
    cols = out.shape[2]
    width = out.shape[3]
    load = pltpu.make_async_copy(slab, straight, local_sem.at[0])
    load.start()

    barrier = pltpu.get_barrier_semaphore()
    for step in range(1, n_vir):
        pl.semaphore_signal(barrier, inc=1, device_id=(o, lax.rem(v + step, n_vir)), device_id_type=MESH)
    for step in range(1, n_occ):
        pl.semaphore_signal(barrier, inc=1, device_id=(lax.rem(o + step, n_occ), v), device_id_type=MESH)
    pl.semaphore_wait(barrier, n_vir + n_occ - 2)

    def place(source, c):
        if c < CHUNKS:
            return gathered.at[source, pl.ds(c * piece, piece)]
        return gathered.at[n_vir, :, pl.ds(pl.multiple_of(source * strip, strip), strip)]

    def held(source, c, own):
        if own and c < CHUNKS:
            return main.at[pl.ds(c * piece, piece)]
        return place(source, c)

    def along(source, c, own, way, target):
        return pltpu.make_async_remote_copy(
            src_ref=held(source, c, own), dst_ref=place(source, c),
            send_sem=send_sem.at[source, c, way], recv_sem=recv_sem.at[source, c],
            device_id=(o, target), device_id_type=MESH,
        )

    def across(source, c, own):
        return pltpu.make_async_remote_copy(
            src_ref=held(source, c, own),
            dst_ref=turned.at[o, lax.rem(source, ratio), pl.ds(c * piece, piece)],
            send_sem=turn_send.at[source, c],
            recv_sem=turn_recv.at[o, lax.rem(source, ratio), c],
            device_id=(source // ratio, v), device_id_type=MESH,
        )

    waits = []

    def start(cond, make):
        def begin():
            make().start()

        def finish():
            make().wait_send()

        pl.when(cond)(begin)
        waits.append((cond, finish))

    def spread(cond, source, c, own, up, down, sides):
        if up:
            start(cond & (z < line - 1), lambda: along(source, c, own, 0, v + wide))
        if down:
            start(cond & (z > 0), lambda: along(source, c, own, 1, v - wide))
        if sides:
            for step in range(1, wide):
                start(cond, lambda step=step: along(source, c, own, 1 + step, z * wide + lax.rem(x + step, wide)))
        if c < CHUNKS:
            start(cond & (source // ratio != o), lambda: across(source, c, own))

    def arrive(cond, source, c, up, down, sides):
        @pl.when(cond)
        def _():
            along(source, c, False, 0, v).wait_recv()

        spread(cond, source, c, False, up, down, sides)

    always = v >= 0

    def permute(part, count):
        swap = pair_swap(STEP)
        across_c = TILE // STEP

        @pl.loop(part * across_c**2 // count, (part + 1) * across_c**2 // count)
        def _(at):
            c = pl.ds(pl.multiple_of(at // across_c * STEP, STEP), STEP)
            d = pl.ds(pl.multiple_of(lax.rem(at, across_c) * STEP, STEP), STEP)
            for n in range(width // WIDE):
                lanes = pl.ds(n * WIDE, WIDE)
                block = straight[c, d, lanes].reshape(STEP * STEP, WIDE)
                moved = jnp.dot(swap, block, preferred_element_type=jnp.float32)
                crossed[d, c, lanes] = moved.astype(jnp.bfloat16).reshape(STEP, STEP, WIDE)

    def multiply(left, weights, places):
        @pl.loop(0, width // NARROW)
        def _(n):
            lanes = pl.ds(pl.multiple_of(n * NARROW, NARROW), NARROW)
            right = weights[:, :, lanes].reshape(cdim, NARROW)
            got = jnp.dot(left(), right, preferred_element_type=jnp.float32)
            for at, (k, source) in enumerate(places):
                rows = got[at * pairs : (at + 1) * pairs].reshape(cols, cols, NARROW)
                out[pl.ds(k * cols, cols), source, :, lanes] = rows.astype(jnp.bfloat16)

    def row_of(occ, vir):
        q, r = vir // ratio, lax.rem(vir, ratio)
        return jnp.where(occ <= q, r, 1 - r)

    def group(zz):
        sources = [zz * wide + step for step in range(wide)]
        multiply(
            lambda: gathered[pl.ds(zz * wide, wide)].reshape(wide * pairs, cdim),
            straight, [(row_of(o, w), w) for w in sources],
        )

    def strip_of(target):
        return extra.at[:, pl.ds(pl.multiple_of(target * strip, strip), strip)]

    own_strip = pltpu.make_async_copy(strip_of(v), place(v, CHUNKS), local_sem.at[1])

    def far_strip(step):
        target = lax.rem(v + step, n_vir)
        return pltpu.make_async_remote_copy(
            src_ref=strip_of(target), dst_ref=place(target, CHUNKS),
            send_sem=extra_send.at[step], recv_sem=recv_sem.at[target, CHUNKS],
            device_id=(o, target), device_id_type=MESH,
        )

    for c in range(CHUNKS):
        spread(always, v, c, True, True, True, True)

    @pl.when(v == owner)
    def _():
        own_strip.start()
        for step in range(1, n_vir):
            far_strip(step).start()
        own_strip.wait()

    gathered[v] = main[...]

    @pl.when(v != owner)
    def _():
        along(v, CHUNKS, False, 0, v).wait_recv()

    spread(always, v, CHUNKS, True, True, True, True)

    for d in range(1, line + 1):
        for c in range(CHUNKS + 1):
            if d < line:
                arrive(z >= d, (z - d) * wide + x, c, True, False, True)
                arrive(z < line - d, (z + d) * wide + x, c, False, True, True)
            for step in range(1, wide):
                side = lax.rem(x + step, wide)
                e = d - 1
                arrive(z >= e, (z - e) * wide + side, c, False, False, False)
                if e:
                    arrive(z < line - e, (z + e) * wide + side, c, False, False, False)
            if d <= 2 and c < CHUNKS:
                if d == 1 and c == 0:
                    load.wait()
                permute((d - 1) * CHUNKS + c, 2 * CHUNKS)
        if d == 1:
            group(z)
        else:
            pl.when(z >= d - 1)(lambda: group(z - d + 1))
            pl.when(z < line - d + 1)(lambda: group(z + d - 1))

    multiply(lambda: gathered[n_vir], straight, [(0, owner)])
    turned[o, 0] = gathered[n_vir]
    for k in range(1, ratio):
        turned[o, k] = gathered[n_vir]
    for step in range(1, n_occ):
        other = lax.rem(o + step, n_occ)
        for k in range(ratio):
            for c in range(CHUNKS):
                pltpu.make_async_remote_copy(
                    src_ref=turned.at[other, k, pl.ds(c * piece, piece)],
                    dst_ref=turned.at[other, k, pl.ds(c * piece, piece)],
                    send_sem=turn_send.at[0, c], recv_sem=turn_recv.at[other, k, c],
                    device_id=(o, v), device_id_type=MESH,
                ).wait_recv()
    swap = pair_swap(cols)

    @pl.loop(0, n_occ * ratio)
    def _(at):
        p, k = at // ratio, lax.rem(at, ratio)
        moved = jnp.dot(swap, turned[p, k], preferred_element_type=jnp.float32)
        turned[p, k] = moved.astype(jnp.bfloat16)

    places = []
    for p in range(n_occ):
        for k in range(ratio):
            s = jnp.where(p < o, k, 1 - k)
            places.append((jnp.where(p == o, 1, k), p * ratio + jnp.where(p == o, 0, s)))
    multiply(lambda: turned[...].reshape(n_occ * ratio * pairs, cdim), crossed, places)
    for cond, finish in waits:
        pl.when(cond)(finish)

    @pl.when(v == owner)
    def _():
        for step in range(1, n_vir):
            far_strip(step).wait_send()


def ladder(n_occ, n_vir, main, extra, slab):
    pairs, cdim = main.shape
    ratio = n_vir // n_occ
    line = LINE if n_vir % LINE == 0 else 1
    wide = n_vir // line
    cols = math.isqrt(pairs)
    return pl.pallas_call(
        functools.partial(exchange_kernel, n_occ, n_vir),
        out_shape=jax.ShapeDtypeStruct((ratio * cols, n_vir, cols, slab.shape[2]), jnp.bfloat16),
        in_specs=[pl.BlockSpec(memory_space=pltpu.VMEM)] * 2 + [pl.BlockSpec(memory_space=pl.ANY)],
        out_specs=pl.BlockSpec(memory_space=pltpu.VMEM),
        scratch_shapes=[
            pltpu.VMEM((n_vir + 1, pairs, cdim), jnp.bfloat16),
            pltpu.VMEM((n_occ, ratio, pairs, cdim), jnp.bfloat16),
            pltpu.VMEM(slab.shape, jnp.bfloat16),
            pltpu.VMEM(slab.shape, jnp.bfloat16),
            pltpu.SemaphoreType.DMA((2,)),
            pltpu.SemaphoreType.DMA((n_vir, CHUNKS + 1, wide + 1)),
            pltpu.SemaphoreType.DMA((n_vir, CHUNKS + 1)),
            pltpu.SemaphoreType.DMA((n_vir, CHUNKS)),
            pltpu.SemaphoreType.DMA((n_occ, ratio, CHUNKS)),
            pltpu.SemaphoreType.DMA((n_vir,)),
        ],
        compiler_params=pltpu.CompilerParams(
            collective_id=0, has_side_effects=True, vmem_limit_bytes=60 * 2**20
        ),
        cost_estimate=pl.CostEstimate(flops=2**35, bytes_accessed=2**25, transcendentals=0),
    )(main, extra, slab)


def flip(block):
    a, b, cdim = block.shape
    return jnp.transpose(block.reshape(a, b, TILE, TILE), (1, 0, 3, 2)).reshape(b, a, cdim)


def add(a, b):
    return (a.astype(jnp.float32) + b.astype(jnp.float32)).astype(jnp.bfloat16)


def per_device(sizes, amplitudes, screen, integrals):
    n_occ, n_vir = sizes
    rows, cols, cdim = amplitudes.shape
    ratio = rows // cols
    assert ratio == 2 and n_vir == ratio * n_occ
    o, v = lax.axis_index("occ"), lax.axis_index("vir")
    q, r = v // ratio, lax.rem(v, ratio)

    def pick(o, q, r):
        return jnp.where(o < q, r, 1 - r)

    parts = (amplitudes * screen[:, :, None].astype(jnp.bfloat16)).reshape(ratio, cols, cols, cdim)

    def half(k):
        return jnp.where(k == 0, parts[0], parts[1])

    pairs = []
    for a in range(n_occ):
        for b in range(n_vir):
            c, s = divmod(b, ratio)
            t = s if c < a else 1 - s
            pairs.append((a * n_vir + b, c * n_vir + a * ratio + t))
    sent = half(jnp.where(q < o, r, 1 - r))
    kept = half(pick(o, q, r))
    cut = cols // PIECES
    sums = []
    for at in range(0, cols, cut):
        got = lax.ppermute(sent[:, at : at + cut], ("occ", "vir"), pairs)
        sums.append(add(kept[at : at + cut], flip(got)))
    mixed = jnp.concatenate(sums)
    inner = add(half(r), flip(half(r)))
    main = jnp.where(o == q, inner, mixed)
    width = integrals.shape[1]
    out = ladder(
        n_occ, n_vir, main.reshape(cols * cols, cdim), mixed.reshape(cols * cols, cdim),
        integrals.reshape(TILE, TILE, width),
    )
    return out.reshape(rows, n_vir * cols, -1, SLAB_VIRT)


def solution(mesh):
    sizes = (mesh.shape["occ"], mesh.shape["vir"])
    return jax.shard_map(
        functools.partial(per_device, sizes),
        mesh=mesh,
        in_specs=(P("occ", "vir", None), P("occ", "vir"), P(None, "vir")),
        out_specs=P("occ", None, "vir", None),
        check_vma=False,
    )
```

```python
import functools
import math

import jax
import jax.numpy as jnp
from jax import lax
from jax.experimental import pallas as pl
from jax.experimental.pallas import tpu as pltpu
from jax.sharding import PartitionSpec as P

TILE = 64
SLAB_VIRT = 128
LINE = 4
CHUNKS = 2
PIECES = 2
PAIR = 2
STEP = 16
WIDE = 512
NARROW = 256
MESH = pl.DeviceIdType.MESH


def pair_swap(n):
    to = lax.broadcasted_iota(jnp.int32, (n * n, n * n), 0)
    at = lax.broadcasted_iota(jnp.int32, (n * n, n * n), 1)
    hit = (lax.rem(to, n) == at // n) & (to // n == lax.rem(at, n))
    return jnp.where(hit, 1.0, 0.0).astype(jnp.bfloat16)


def exchange_kernel(
    n_occ, n_vir, main, extra, slab, out, gathered, turned, straight, crossed,
    local_sem, send_sem, recv_sem, turn_send, turn_recv, extra_send,
):
    ratio = n_vir // n_occ
    line = LINE if n_vir % LINE == 0 else 1
    wide = n_vir // line
    o, v = lax.axis_index("occ"), lax.axis_index("vir")
    z, x = v // wide, lax.rem(v, wide)
    pairs, cdim = main.shape
    piece = pairs // CHUNKS
    strip = cdim // n_vir
    owner = o * ratio + 1
    cols = out.shape[2]
    width = out.shape[3]
    load = pltpu.make_async_copy(slab, straight, local_sem.at[0])
    load.start()

    barrier = pltpu.get_barrier_semaphore()
    for step in range(1, n_vir):
        pl.semaphore_signal(barrier, inc=1, device_id=(o, lax.rem(v + step, n_vir)), device_id_type=MESH)
    for step in range(1, n_occ):
        pl.semaphore_signal(barrier, inc=1, device_id=(lax.rem(o + step, n_occ), v), device_id_type=MESH)
    pl.semaphore_wait(barrier, n_vir + n_occ - 2)

    def place(source, c):
        if c < CHUNKS:
            return gathered.at[source, pl.ds(c * piece, piece)]
        return gathered.at[n_vir, :, pl.ds(pl.multiple_of(source * strip, strip), strip)]

    def held(source, c, own):
        if own and c < CHUNKS:
            return main.at[pl.ds(c * piece, piece)]
        return place(source, c)

    def along(source, c, own, way, target):
        return pltpu.make_async_remote_copy(
            src_ref=held(source, c, own), dst_ref=place(source, c),
            send_sem=send_sem.at[source, c, way], recv_sem=recv_sem.at[source, c],
            device_id=(o, target), device_id_type=MESH,
        )

    def across(source, c, own):
        return pltpu.make_async_remote_copy(
            src_ref=held(source, c, own),
            dst_ref=turned.at[o, lax.rem(source, ratio), pl.ds(c * piece, piece)],
            send_sem=turn_send.at[source, c],
            recv_sem=turn_recv.at[o, lax.rem(source, ratio), c],
            device_id=(source // ratio, v), device_id_type=MESH,
        )

    waits = []

    def start(cond, make):
        def begin():
            make().start()

        def finish():
            make().wait_send()

        pl.when(cond)(begin)
        waits.append((cond, finish))

    def spread(cond, source, c, own, up, down, sides):
        if up:
            start(cond & (z < line - 1), lambda: along(source, c, own, 0, v + wide))
        if down:
            start(cond & (z > 0), lambda: along(source, c, own, 1, v - wide))
        if sides:
            for step in range(1, wide):
                start(cond, lambda step=step: along(source, c, own, 1 + step, z * wide + lax.rem(x + step, wide)))
        if c < CHUNKS:
            start(cond & (source // ratio != o), lambda: across(source, c, own))

    def arrive(cond, source, c, up, down, sides):
        @pl.when(cond)
        def _():
            along(source, c, False, 0, v).wait_recv()

        spread(cond, source, c, False, up, down, sides)

    always = v >= 0

    def permute(part, count):
        swap = pair_swap(STEP)
        across_c = TILE // STEP

        @pl.loop(part * across_c**2 // count, (part + 1) * across_c**2 // count)
        def _(at):
            c = pl.ds(pl.multiple_of(at // across_c * STEP, STEP), STEP)
            d = pl.ds(pl.multiple_of(lax.rem(at, across_c) * STEP, STEP), STEP)
            for n in range(width // WIDE):
                lanes = pl.ds(n * WIDE, WIDE)
                block = straight[c, d, lanes].reshape(STEP * STEP, WIDE)
                moved = jnp.dot(swap, block, preferred_element_type=jnp.float32)
                crossed[d, c, lanes] = moved.astype(jnp.bfloat16).reshape(STEP, STEP, WIDE)

    def multiply(left, weights, places):
        @pl.loop(0, width // NARROW)
        def _(n):
            lanes = pl.ds(pl.multiple_of(n * NARROW, NARROW), NARROW)
            right = weights[:, :, lanes].reshape(cdim, NARROW)
            got = jnp.dot(left(), right, preferred_element_type=jnp.float32)
            for at, (k, source) in enumerate(places):
                rows = got[at * pairs : (at + 1) * pairs].reshape(cols, cols, NARROW)
                out[pl.ds(k * cols, cols), source, :, lanes] = rows.astype(jnp.bfloat16)

    def row_of(occ, vir):
        q, r = vir // ratio, lax.rem(vir, ratio)
        return jnp.where(occ <= q, r, 1 - r)

    def group(zz):
        sources = [zz * wide + step for step in range(wide)]
        multiply(
            lambda: gathered[pl.ds(zz * wide, wide)].reshape(wide * pairs, cdim),
            straight, [(row_of(o, w), w) for w in sources],
        )

    def strip_of(target):
        return extra.at[:, pl.ds(pl.multiple_of(target * strip, strip), strip)]

    own_strip = pltpu.make_async_copy(strip_of(v), place(v, CHUNKS), local_sem.at[1])

    def far_strip(step):
        target = lax.rem(v + step, n_vir)
        return pltpu.make_async_remote_copy(
            src_ref=strip_of(target), dst_ref=place(target, CHUNKS),
            send_sem=extra_send.at[step], recv_sem=recv_sem.at[target, CHUNKS],
            device_id=(o, target), device_id_type=MESH,
        )

    @pl.when(v == owner)
    def _():
        own_strip.start()
        for step in range(1, n_vir):
            far_strip(step).start()

    for c in range(CHUNKS):
        spread(always, v, c, True, True, True, True)
    gathered[v] = main[...]

    def phase(d, c):
        if d < line:
            arrive(z >= d, (z - d) * wide + x, c, True, False, True)
            arrive(z < line - d, (z + d) * wide + x, c, False, True, True)
        e = d - 1
        for step in range(1, wide):
            side = lax.rem(x + step, wide)
            arrive(z >= e, (z - e) * wide + side, c, False, False, False)
            if e:
                arrive(z < line - e, (z + e) * wide + side, c, False, False, False)

    for d in range(1, line + 1):
        for c in range(CHUNKS):
            phase(d, c)
            if d <= 2:
                if d == 1 and c == 0:
                    load.wait()
                permute((d - 1) * CHUNKS + c, 2 * CHUNKS)
        if d == 1:
            pl.when(v == owner)(own_strip.wait)

            @pl.when(v != owner)
            def _():
                along(v, CHUNKS, False, 0, v).wait_recv()

            spread(always, v, CHUNKS, True, True, True, True)
            group(z)
        else:
            phase(d - 1, CHUNKS)
            pl.when(z >= d - 1)(lambda: group(z - d + 1))
            pl.when(z < line - d + 1)(lambda: group(z + d - 1))
    phase(line, CHUNKS)

    multiply(lambda: gathered[n_vir], straight, [(0, owner)])
    turned[o, 0] = gathered[n_vir]
    for k in range(1, ratio):
        turned[o, k] = gathered[n_vir]
    swap = pair_swap(cols)
    for step in range(n_occ // PAIR):
        base = lax.rem(o // PAIR + step, n_occ // PAIR) * PAIR
        places = []
        for p in [base + at for at in range(PAIR)]:
            for k in range(ratio):

                @pl.when(p != o)
                def _(p=p, k=k):
                    for c in range(CHUNKS):
                        landed = turned.at[p, k, pl.ds(c * piece, piece)]
                        pltpu.make_async_remote_copy(
                            src_ref=landed, dst_ref=landed,
                            send_sem=turn_send.at[0, c], recv_sem=turn_recv.at[p, k, c],
                            device_id=(o, v), device_id_type=MESH,
                        ).wait_recv()

                moved = jnp.dot(swap, turned[p, k], preferred_element_type=jnp.float32)
                turned[p, k] = moved.astype(jnp.bfloat16)
                s = jnp.where(p < o, k, 1 - k)
                places.append((jnp.where(p == o, 1, k), p * ratio + jnp.where(p == o, 0, s)))
        multiply(
            lambda base=base: turned[pl.ds(base, PAIR)].reshape(PAIR * ratio * pairs, cdim),
            crossed, places,
        )
    for cond, finish in waits:
        pl.when(cond)(finish)

    @pl.when(v == owner)
    def _():
        for step in range(1, n_vir):
            far_strip(step).wait_send()


def ladder(n_occ, n_vir, main, extra, slab):
    pairs, cdim = main.shape
    ratio = n_vir // n_occ
    line = LINE if n_vir % LINE == 0 else 1
    wide = n_vir // line
    cols = math.isqrt(pairs)
    return pl.pallas_call(
        functools.partial(exchange_kernel, n_occ, n_vir),
        out_shape=jax.ShapeDtypeStruct((ratio * cols, n_vir, cols, slab.shape[2]), jnp.bfloat16),
        in_specs=[pl.BlockSpec(memory_space=pltpu.VMEM)] * 2 + [pl.BlockSpec(memory_space=pl.ANY)],
        out_specs=pl.BlockSpec(memory_space=pltpu.VMEM),
        scratch_shapes=[
            pltpu.VMEM((n_vir + 1, pairs, cdim), jnp.bfloat16),
            pltpu.VMEM((n_occ, ratio, pairs, cdim), jnp.bfloat16),
            pltpu.VMEM(slab.shape, jnp.bfloat16),
            pltpu.VMEM(slab.shape, jnp.bfloat16),
            pltpu.SemaphoreType.DMA((2,)),
            pltpu.SemaphoreType.DMA((n_vir, CHUNKS + 1, wide + 1)),
            pltpu.SemaphoreType.DMA((n_vir, CHUNKS + 1)),
            pltpu.SemaphoreType.DMA((n_vir, CHUNKS)),
            pltpu.SemaphoreType.DMA((n_occ, ratio, CHUNKS)),
            pltpu.SemaphoreType.DMA((n_vir,)),
        ],
        compiler_params=pltpu.CompilerParams(
            collective_id=0, has_side_effects=True, vmem_limit_bytes=60 * 2**20
        ),
        cost_estimate=pl.CostEstimate(flops=2**35, bytes_accessed=2**25, transcendentals=0),
    )(main, extra, slab)


def flip(block):
    a, b, cdim = block.shape
    return jnp.transpose(block.reshape(a, b, TILE, TILE), (1, 0, 3, 2)).reshape(b, a, cdim)


def add(a, b):
    return (a.astype(jnp.float32) + b.astype(jnp.float32)).astype(jnp.bfloat16)


def per_device(sizes, amplitudes, screen, integrals):
    n_occ, n_vir = sizes
    rows, cols, cdim = amplitudes.shape
    ratio = rows // cols
    assert ratio == 2 and n_vir == ratio * n_occ
    o, v = lax.axis_index("occ"), lax.axis_index("vir")
    q, r = v // ratio, lax.rem(v, ratio)

    def pick(o, q, r):
        return jnp.where(o < q, r, 1 - r)

    parts = (amplitudes * screen[:, :, None].astype(jnp.bfloat16)).reshape(ratio, cols, cols, cdim)

    def half(k):
        return jnp.where(k == 0, parts[0], parts[1])

    pairs = []
    for a in range(n_occ):
        for b in range(n_vir):
            c, s = divmod(b, ratio)
            t = s if c < a else 1 - s
            pairs.append((a * n_vir + b, c * n_vir + a * ratio + t))
    sent = half(jnp.where(q < o, r, 1 - r))
    kept = half(pick(o, q, r))
    cut = cols // PIECES
    sums = []
    for at in range(0, cols, cut):
        got = lax.ppermute(sent[:, at : at + cut], ("occ", "vir"), pairs)
        sums.append(add(kept[at : at + cut], flip(got)))
    mixed = jnp.concatenate(sums)
    inner = add(half(r), flip(half(r)))
    main = jnp.where(o == q, inner, mixed)
    width = integrals.shape[1]
    out = ladder(
        n_occ, n_vir, main.reshape(cols * cols, cdim), mixed.reshape(cols * cols, cdim),
        integrals.reshape(TILE, TILE, width),
    )
    return out.reshape(rows, n_vir * cols, -1, SLAB_VIRT)


def solution(mesh):
    sizes = (mesh.shape["occ"], mesh.shape["vir"])
    return jax.shard_map(
        functools.partial(per_device, sizes),
        mesh=mesh,
        in_specs=(P("occ", "vir", None), P("occ", "vir"), P(None, "vir")),
        out_specs=P("occ", None, "vir", None),
        check_vma=False,
    )
```
